128 devices in a mesh: dp: 8 (over z, core), seq: 16 (over x, y).
Axes of the slice: x: 4, y: 4, z: 4, core: 2. Of those that a mesh axis runs over, the one named last changes fastest.
Arguments:
- queries: bfloat16 [16, 16, 512, 1536], P('dp', 'seq'), may hold values from -18 to 18
- key_rows: bfloat16 [16, 16, 512, 1536], P('dp', 'seq'), may hold values from -4 to 4
- value_rows: bfloat16 [16, 16, 512, 1536], P('dp', 'seq'), may hold values from -6 to 6
- cotangent: bfloat16 [16, 16, 512, 1536], P('dp', 'seq'), may hold values from -6 to 6
- frame_counts: int32 [16], replicated, may hold values from 9 to 16
- patch_rows: int32 [16], replicated, may hold values from 10 to 16
- patch_cols: int32 [16], replicated, may hold values from 20 to 32
- swap_flags: int32 [4, 2], replicated, may hold values from 0 to 1, as said below
Outputs:
- block_out: bfloat16 [16, 16, 512, 1536], P('dp', 'seq')
- grad_queries: bfloat16 [16, 16, 512, 1536], P('dp', 'seq')
- grad_keys: bfloat16 [16, 16, 512, 1536], P('dp', 'seq')
- grad_values: bfloat16 [16, 16, 512, 1536], P('dp', 'seq')
The draws below stay inside these ranges and needn't reach their ends.
Inputs may be any that keep to these rules, and one draw needn't show every extreme that they name: `swap_flags`: in every draw some clip is traded and some clip is not.
All inputs are finite; a program needn't handle non-finite values.
Results may differ from the reference program's by a relative error of at most 0.0058.
Values may be sent and summed in bfloat16 or wider, within the bound.
A program may use at most 256 MiB of HBM per device.

```python
import jax
import jax.numpy as jnp
from jax import lax

HEADS = 12
HEAD_DIM = 128
WIDTH = 1536
SLOTS = 2
FRAMES = 16
GRID_H = 16
GRID_W = 32
CELLS = 512
CLIPS = 16
PAIRS = 4


def draw_queries(key, part):
    key = jax.random.fold_in(key, 1)
    full_shape = (CLIPS, FRAMES, CELLS, HEADS * HEAD_DIM)
    return jax.random.truncated_normal(key, -4.0, 4.0, full_shape, jnp.float32).astype(jnp.bfloat16)


def draw_key_rows(key, part):
    key = jax.random.fold_in(key, 2)
    full_shape = (CLIPS, FRAMES, CELLS, HEADS * HEAD_DIM)
    return jax.random.truncated_normal(key, -4.0, 4.0, full_shape, jnp.float32).astype(jnp.bfloat16)


def draw_swap_flags(key, part):
    key = jax.random.fold_in(key, 3)
    bit_key, chosen_key, step_key = jax.random.split(key, 3)
    entry_count = PAIRS * SLOTS
    flag_bits = jax.random.randint(bit_key, (entry_count,), 0, 2)
    chosen = jax.random.randint(chosen_key, (), 0, entry_count)
    kept_entry = (chosen + 1 + jax.random.randint(step_key, (), 0, entry_count - 1)) % entry_count
    flag_bits = flag_bits.at[chosen].set(1).at[kept_entry].set(0)
    return flag_bits.reshape(PAIRS, SLOTS).astype(jnp.int32)


def with_ends(array, stream_key, smallest, largest):
    index_at = [jax.random.randint(jax.random.fold_in(stream_key, axis), (), 0, length) for axis, length in enumerate(array.shape)]
    widest = array.shape.index(max(array.shape))
    neighbour = index_at[:widest] + [(index_at[widest] + 1) % array.shape[widest]] + index_at[widest + 1:]
    return array.at[tuple(index_at)].set(smallest).at[tuple(neighbour)].set(largest)


def steps_of(own_key, extent, pieces, smallest, top_value):
    loudness = 1.0
    for axis_at, shards_of in pieces:
        steps = jax.random.uniform(jax.random.fold_in(jax.random.fold_in(own_key, 6), axis_at), (shards_of,), jnp.float32, smallest / len(pieces), top_value / len(pieces))
        loudness = loudness * jnp.repeat(jnp.exp(steps), extent[axis_at] // shards_of).reshape((-1,) + (1,) * (len(extent) - 1 - axis_at))
    return loudness


def bell_draw(own_key, extent, spread, bound, cuts=(), held_as=jnp.bfloat16):
    result = spread * jax.random.normal(own_key, extent, jnp.float32)
    if cuts:
        result = result * steps_of(own_key, extent, cuts, -0.22, 0.18)
    return jnp.clip(result, -bound, bound).astype(held_as)


def setup_inputs(seed: int = 0) -> dict:
    key_list = jax.random.split(jax.random.key(seed), 9)
    queries = draw_queries(jax.random.fold_in(key_list[8], 71), 0)
    key_rows = draw_key_rows(jax.random.fold_in(key_list[8], 71), 0)
    value_rows = bell_draw(key_list[2], (CLIPS, FRAMES, CELLS, WIDTH), 1.0, 6.0, ((0, 8), (1, 16)))
    cotangent = bell_draw(key_list[3], (CLIPS, FRAMES, CELLS, WIDTH), 1.0, 6.0, ((0, 8), (1, 16)))
    frame_counts = with_ends(jax.random.randint(key_list[4], (CLIPS,), FRAMES // 2 + 1, FRAMES + 1), jax.random.fold_in(key_list[4], 1), FRAMES // 2 + 1, FRAMES).astype(jnp.int32)
    patch_rows = with_ends(jax.random.randint(key_list[5], (CLIPS,), GRID_H * 5 // 8, GRID_H + 1), jax.random.fold_in(key_list[5], 1), GRID_H * 5 // 8, GRID_H).astype(jnp.int32)
    patch_cols = with_ends(jax.random.randint(key_list[6], (CLIPS,), max(2, GRID_W * 5 // 8), GRID_W + 1), jax.random.fold_in(key_list[6], 1), max(2, GRID_W * 5 // 8), GRID_W).astype(jnp.int32)
    swap_flags = draw_swap_flags(jax.random.fold_in(key_list[8], 71), 0)
    return dict(queries=queries, key_rows=key_rows, value_rows=value_rows, cotangent=cotangent, frame_counts=frame_counts, patch_rows=patch_rows, patch_cols=patch_cols, swap_flags=swap_flags)


masked_score = -1e30


def attention(queries, key_rows, value_rows, cotangent, key_mask, row_mask, einsum_forms):
    score_form, mix_form, back_form = einsum_forms
    scale = HEAD_DIM ** -0.5
    scores = jnp.einsum(score_form, queries.astype(jnp.float32), key_rows.astype(jnp.float32)) * scale
    scores = jnp.where(key_mask, scores, masked_score)
    row_max = jnp.max(scores, axis=-1, keepdims=True)
    exponent = jnp.exp(scores - row_max)
    softmax = exponent / jnp.sum(exponent, axis=-1, keepdims=True)
    weights = lax.optimization_barrier(softmax.astype(jnp.bfloat16))
    masked_grad = jnp.where(row_mask, cotangent, jnp.zeros_like(cotangent))
    attended = jnp.einsum(mix_form, weights.astype(jnp.float32), value_rows.astype(jnp.float32))
    grad_value = jnp.einsum(back_form, weights.astype(jnp.float32), masked_grad.astype(jnp.float32))
    grad_weight = jnp.einsum(score_form, masked_grad.astype(jnp.float32), value_rows.astype(jnp.float32))
    row_dot = jnp.sum(softmax * grad_weight, axis=-1, keepdims=True)
    grad_score = lax.optimization_barrier((softmax * (grad_weight - row_dot) * scale).astype(jnp.bfloat16))
    grad_query = jnp.einsum(mix_form, grad_score.astype(jnp.float32), key_rows.astype(jnp.float32))
    grad_key = jnp.einsum(back_form, grad_score.astype(jnp.float32), queries.astype(jnp.float32))
    attended = jnp.where(row_mask, attended, jnp.zeros_like(attended))
    return attended, grad_query, grad_key, grad_value


def clip_block(clip_items):
    queries, key_rows, value_rows, cotangent, frame_count, rows_seen, cols_seen = clip_items
    split_shape = (FRAMES, CELLS, HEADS, HEAD_DIM)
    query_heads = queries.reshape(split_shape)
    key_heads = key_rows.reshape(split_shape)
    value_heads = value_rows.reshape(split_shape)
    grad_heads = cotangent.reshape(split_shape)
    frame_ids = jnp.arange(FRAMES)[:, None]
    cell_ids = jnp.arange(CELLS)[None, :]
    inside = (frame_ids < frame_count) & (cell_ids // GRID_W < rows_seen) & (cell_ids % GRID_W < cols_seen)
    spatial_forms = ("lhe,mhe->hlm", "hlm,mhe->lhe", "hlm,lhe->mhe")

    def one_frame(frame_items):
        frame_query, frame_keys, frame_values, frame_grad, frame_inside = frame_items
        return attention(frame_query, frame_keys, frame_values, frame_grad,
                         frame_inside[None, None, :], frame_inside[:, None, None], spatial_forms)

    spatial_part = lax.map(one_frame, (query_heads, key_heads, value_heads, grad_heads, inside))
    temporal_forms = ("lbhe,mbhe->bhlm", "bhlm,mbhe->lbhe", "bhlm,lbhe->mbhe")
    temporal_part = attention(query_heads, key_heads, value_heads, grad_heads,
                              inside.T[:, None, None, :], inside[:, :, None, None], temporal_forms)
    results = []
    for spatial_piece, temporal_piece in zip(spatial_part, temporal_part):
        rounded = lax.optimization_barrier(temporal_piece.astype(jnp.bfloat16))
        summed = spatial_piece + rounded.astype(jnp.float32)
        results.append(summed.astype(jnp.bfloat16).reshape(FRAMES, CELLS, HEADS * HEAD_DIM))
    return tuple(results)


def reference(queries, key_rows, value_rows, cotangent, frame_counts, patch_rows, patch_cols, swap_flags):
    clip_ids = jnp.arange(CLIPS, dtype=jnp.int32)
    group_ids = clip_ids // SLOTS
    slot_ids = clip_ids % SLOTS
    swapped = swap_flags[group_ids % PAIRS, slot_ids] == 1
    partner_ids = jnp.bitwise_xor(group_ids, PAIRS) * SLOTS + slot_ids
    source = jnp.where(swapped, partner_ids, clip_ids).astype(jnp.int32)
    moved = (queries[source], key_rows[source], value_rows[source], cotangent,
             frame_counts[source], patch_rows[source], patch_cols[source])
    results = lax.map(clip_block, moved)
    return results[0], results[1], results[2], results[3]
```

```python
import functools

import jax
import jax.numpy as jnp
from jax import lax
from jax.experimental import pallas as pl
from jax.experimental.pallas import tpu as pltpu
from jax.sharding import PartitionSpec as P

HEAD_DIM = 128
GRID_W = 32
CELLS = 512
FRAMES = 16
SLOTS = 2
WIDTH = 1536
PACK = 2 * HEAD_DIM
CHUNKS = WIDTH // PACK
SCALE = HEAD_DIM**-0.5
LOG2E = 1.4426950408889634
MASKED = -1e30
MESH = pl.DeviceIdType.MESH
BF16 = jnp.bfloat16
F32 = jnp.float32
LAG_TIME = 1
LAG_SPACE = 2
OFFSETS = (
    (1, 0), (3, 0), (0, 1), (0, 3), (1, 1), (3, 3), (1, 3), (3, 1),
    (2, 0), (0, 2), (2, 2), (1, 2), (3, 2), (2, 1), (2, 3),
)


def dot(a, b, dims):
    return lax.dot_general(a, b, (dims, ((), ())), preferred_element_type=F32)


def attend(q, k, v, g, bias):
    s = dot(q, k, ((1,), (1,))) * (SCALE * LOG2E) + bias
    e = jnp.exp2(s - jnp.max(s, axis=-1, keepdims=True))
    p = e * (1.0 / jnp.sum(e, axis=-1, keepdims=True))
    pb = p.astype(BF16)
    o = dot(pb, v, ((1,), (0,)))
    dv = dot(pb, g, ((0,), (0,)))
    dp = dot(g, v, ((1,), (1,)))
    row_dot = jnp.sum(p * dp, axis=-1, keepdims=True)
    ds = (p * (dp - row_dot) * SCALE).astype(BF16)
    dq = dot(ds, k, ((1,), (0,)))
    dk = dot(ds, q, ((0,), (0,)))
    return o, dq, dk, dv


def block_kernel(
    n,
    q_hbm, k_hbm, v_hbm, g_hbm,
    pack_ref, unpack_ref, swap_ref, row_ref, space_bias, time_bias, diag_ref,
    o_hbm, dq_hbm, dk_hbm, dv_hbm,
    moved, own, grad, grad_out, stage, work, back, space, result,
    z_send, z_recv, own_sem, grad_sem, gs_send, f_send, f_recv, b_send, b_recv, out_sem,
):
    rows = 2 * n
    cap = 16 * n
    me = lax.axis_index("seq")
    group = lax.axis_index("dp")
    partner = lax.rem(group + 4, 8)
    mx, my = me // 4, lax.rem(me, 4)
    peers = [lax.rem(mx + ox, 4) * 4 + lax.rem(my + oy, 4) for ox, oy in OFFSETS]
    homes = (q_hbm, k_hbm, v_hbm)
    outs = (o_hbm, dq_hbm, dk_hbm, dv_hbm)

    def columns(i):
        return pl.ds(pl.multiple_of(i * PACK, PACK), PACK)

    def own_copies(i):
        return [
            pltpu.make_async_copy(
                homes[a].at[:, :, columns(i)], own.at[lax.rem(i, 2), a], own_sem.at[lax.rem(i, 2)]
            )
            for a in range(3)
        ]

    def z_copies(i):
        return [
            pltpu.make_async_remote_copy(
                src_ref=homes[a].at[:, :, columns(i)],
                dst_ref=moved.at[i, a],
                send_sem=z_send.at[i],
                recv_sem=z_recv.at[i],
                device_id={"dp": partner},
                device_id_type=MESH,
            )
            for a in range(3)
        ]

    def start(copies):
        for copy in copies:
            copy.start()

    def wait_bytes(ref, sem):
        pltpu.make_async_copy(ref, ref, sem).wait()

    def packed(values):
        taken = dot(pack_ref[...], values, ((1,), (0,)))
        parts = [taken[:, b * 128 : (b + 1) * 128].reshape(16, n, 128) for b in range(2)]
        return jnp.concatenate(parts, axis=1).astype(BF16)

    barrier = pltpu.get_barrier_semaphore()
    for peer in peers:
        pl.semaphore_signal(barrier, inc=1, device_id={"seq": peer}, device_id_type=MESH)
    pl.semaphore_signal(barrier, inc=1, device_id={"dp": partner}, device_id_type=MESH)

    def load_grad(i, _):
        pltpu.make_async_copy(g_hbm.at[:, :, columns(i)], grad.at[i], grad_sem.at[i]).start()
        return 0

    lax.fori_loop(0, CHUNKS, load_grad, 0)
    start(own_copies(0))
    start(own_copies(1))
    pl.semaphore_wait(barrier, 16)
    start(z_copies(0))
    start(z_copies(1))

    def send_grad(i, _):
        wait_bytes(grad.at[i], grad_sem.at[i])
        grad_out[i] = packed(grad[i].reshape(SLOTS * CELLS, PACK))
        for peer in peers:
            pltpu.make_async_remote_copy(
                src_ref=grad_out.at[i, peer],
                dst_ref=work.at[i, me, 3],
                send_sem=gs_send.at[i],
                recv_sem=f_recv.at[i],
                device_id={"seq": peer},
                device_id_type=MESH,
            ).start()
        work[i, me, 3] = grad_out[i, me]
        return 0

    lax.fori_loop(0, CHUNKS, send_grad, 0)

    def send_chunk(i):
        slot = lax.rem(i, 2)
        wait_bytes(own.at[slot], own_sem.at[slot])
        wait_bytes(moved.at[i], z_recv.at[i])

        @pl.when(i + 2 < CHUNKS)
        def _():
            start(z_copies(i + 2))

        @pl.when(i >= 2)
        def _():
            wait_bytes(stage.at[slot, pl.ds(0, 15)], f_send.at[slot])

        for a in range(3):
            for s in range(SLOTS):
                moved[i, a, s] = jnp.where(swap_ref[s, 0:1, :] > 0, moved[i, a, s], own[slot, a, s])
            stage[slot, :, a] = packed(moved[i, a].reshape(SLOTS * CELLS, PACK))

        @pl.when(i + 2 < CHUNKS)
        def _():
            start(own_copies(i + 2))

        for peer in peers:
            pltpu.make_async_remote_copy(
                src_ref=stage.at[slot, peer],
                dst_ref=work.at[i, me, pl.ds(0, 3)],
                send_sem=f_send.at[slot],
                recv_sem=f_recv.at[i],
                device_id={"seq": peer},
                device_id_type=MESH,
            ).start()
        work[i, me, pl.ds(0, 3)] = stage[slot, me]

    def time_chunk(i):
        wait_bytes(work.at[i, pl.ds(0, 15)], f_recv.at[i])

        def one(r, _):
            at = pl.ds(pl.multiple_of(r * 16, 16), 16)
            q, k, v, g = [work[i, :, a, at, :].reshape(256, 128) for a in range(4)]
            bias = diag_ref[...] + time_bias[r, 0:1, :]
            for a, value in enumerate(attend(q, k, v, g, bias)):
                work[i, :, a, at, :] = value.astype(BF16).reshape(16, 16, 128)
            return 0

        lax.fori_loop(0, rows // 16, one, 0)
        for peer in peers:
            pltpu.make_async_remote_copy(
                src_ref=work.at[i, peer],
                dst_ref=back.at[i, me],
                send_sem=b_send.at[i],
                recv_sem=b_recv.at[i],
                device_id={"seq": peer},
                device_id_type=MESH,
            ).start()
        back[i, me] = work[i, me]

    def space_chunk(i):
        def one(step, _):
            s, b = step // 2, lax.rem(step, 2)
            lanes = pl.ds(pl.multiple_of(b * 128, 128), 128)
            q, k, v = [moved[i, a, s, :, lanes] for a in range(3)]
            seen = row_ref[s]
            g = grad[i, s, :, lanes] * seen
            o, dq, dk, dv = attend(q, k, v, g, space_bias[s, 0:1, :])
            o = o * seen.astype(F32)
            for a, value in enumerate((o, dq, dk, dv)):
                space[a, s, :, lanes] = value
            return 0

        lax.fori_loop(0, 2 * SLOTS, one, 0)
        wait_bytes(back.at[i, pl.ds(0, 15)], b_recv.at[i])

        @pl.when(i > 0)
        def _():
            wait_bytes(result, out_sem)

        for a in range(4):
            value = back[i, :, a].astype(F32)
            parts = [value[:, b * n : (b + 1) * n].reshape(cap, 128) for b in range(2)]
            taken = dot(unpack_ref[...], jnp.concatenate(parts, axis=1).astype(BF16), ((1,), (0,)))
            summed = space[a].reshape(SLOTS * CELLS, PACK) + taken
            result[a] = summed.astype(BF16).reshape(SLOTS, CELLS, PACK)
        start(
            [
                pltpu.make_async_copy(result.at[a], outs[a].at[:, :, columns(i)], out_sem)
                for a in range(4)
            ]
        )

    def step(i, _):
        @pl.when(i < CHUNKS)
        def _():
            send_chunk(i)

        @pl.when((i >= LAG_TIME) & (i < CHUNKS + LAG_TIME))
        def _():
            time_chunk(i - LAG_TIME)

        @pl.when(i >= LAG_SPACE)
        def _():
            space_chunk(i - LAG_SPACE)

        return 0

    lax.fori_loop(0, CHUNKS + LAG_SPACE, step, 0)
    wait_bytes(result, out_sem)

    def finish(i, _):
        wait_bytes(moved.at[i], z_send.at[i])
        wait_bytes(grad_out.at[i, pl.ds(0, 15)], gs_send.at[i])
        wait_bytes(work.at[i, pl.ds(0, 15)], b_send.at[i])
        return 0

    lax.fori_loop(0, CHUNKS, finish, 0)
    for slot in range(2):
        wait_bytes(stage.at[slot, pl.ds(0, 15)], f_send.at[slot])


def pick(table, ids):
    match = ids[:, None] == jnp.arange(table.shape[0])[None, :]
    return jnp.sum(jnp.where(match, table[None, :], 0), axis=1)


def run_block(n, q, k, v, g, swaps, counts, seen_rows, seen_cols):
    rows, cap = 2 * n, 16 * n
    frame = lax.axis_index("seq")
    cells = jnp.arange(CELLS)
    y, x = cells // GRID_W, cells % GRID_W
    inside = (y[None] < seen_rows[:, None]) & (x[None] < seen_cols[:, None])
    areas = seen_rows * seen_cols
    place = y[None] * seen_cols[:, None] + x[None] + jnp.array([0, 1])[:, None] * areas[0]
    live = inside & (frame < counts)[:, None]
    place = jnp.where(live, place, -1).reshape(-1)
    pack = (jnp.arange(cap)[:, None] == place[None, :]).astype(BF16)
    unpack = (place[:, None] == jnp.arange(cap)[None, :]).astype(BF16)
    swap = jnp.broadcast_to(swaps.astype(BF16)[:, None, None], (SLOTS, 16, PACK))
    row = jnp.broadcast_to(live.astype(BF16)[:, :, None], (SLOTS, CELLS, 128))
    space_bias = jnp.where(live, 0.0, MASKED).astype(F32)
    space_bias = jnp.broadcast_to(space_bias[:, None, :], (SLOTS, 8, CELLS))
    cell = frame * n + jnp.arange(rows) % n
    cell_count = jnp.where(cell < areas[0], counts[0], counts[1])
    cell_count = jnp.where(cell < areas[0] + areas[1], cell_count, FRAMES)
    alive = jnp.arange(FRAMES)[None, :, None] < cell_count.reshape(rows // 16, 1, 16)
    time_bias = jnp.where(alive, 0.0, MASKED).astype(F32).reshape(rows // 16, 1, 256)
    time_bias = jnp.broadcast_to(time_bias, (rows // 16, 8, 256))
    token = jnp.arange(256) % 16
    diag = jnp.where(token[:, None] == token[None, :], 0.0, MASKED).astype(F32)

    shape = (SLOTS, CELLS, WIDTH)
    whole = pl.BlockSpec(memory_space=pl.ANY)
    local = pl.BlockSpec(memory_space=pltpu.VMEM)
    dma = pltpu.SemaphoreType.DMA
    outs = pl.pallas_call(
        functools.partial(block_kernel, n),
        out_shape=[jax.ShapeDtypeStruct(shape, BF16)] * 4,
        in_specs=[whole] * 4 + [local] * 7,
        out_specs=[whole] * 4,
        scratch_shapes=[
            pltpu.VMEM((CHUNKS, 3, SLOTS, CELLS, PACK), BF16),
            pltpu.VMEM((2, 3, SLOTS, CELLS, PACK), BF16),
            pltpu.VMEM((CHUNKS, SLOTS, CELLS, PACK), BF16),
            pltpu.VMEM((CHUNKS, 16, rows, 128), BF16),
            pltpu.VMEM((2, 16, 3, rows, 128), BF16),
            pltpu.VMEM((CHUNKS, 16, 4, rows, 128), BF16),
            pltpu.VMEM((CHUNKS, 16, 4, rows, 128), BF16),
            pltpu.VMEM((4, SLOTS, CELLS, PACK), F32),
            pltpu.VMEM((4, SLOTS, CELLS, PACK), BF16),
            dma((CHUNKS,)),
            dma((CHUNKS,)),
            dma((2,)),
            dma((CHUNKS,)),
            dma((CHUNKS,)),
            dma((2,)),
            dma((CHUNKS,)),
            dma((CHUNKS,)),
            dma((CHUNKS,)),
            dma,
        ],
        compiler_params=pltpu.CompilerParams(
            collective_id=n // 8, has_side_effects=True, vmem_limit_bytes=63 * 2**20
        ),
        cost_estimate=pl.CostEstimate(
            flops=2 * 10**10, bytes_accessed=24 * 2**20, transcendentals=10**7
        ),
    )(
        *[value.reshape(shape) for value in (q, k, v, g)],
        pack, unpack, swap, row, space_bias, time_bias, diag,
    )
    return tuple(value.reshape(SLOTS, 1, CELLS, WIDTH) for value in outs)


SIZES = (48, 56, 64)


def shards(q, k, v, g, frame_counts, patch_rows, patch_cols, swap_flags):
    group = lax.axis_index("dp")
    clips = jnp.arange(16)
    swapped = pick(swap_flags.reshape(-1), (clips // 2 % 4) * 2 + clips % 2) == 1
    source = jnp.where(swapped, clips ^ 8, clips)
    home = group * 2 + jnp.arange(2)
    counts, seen_rows, seen_cols = [
        pick(pick(table, source), home) for table in (frame_counts, patch_rows, patch_cols)
    ]
    swaps = pick(swapped.astype(jnp.int32), home)
    needed = jnp.max(jnp.sum(pick(patch_rows * patch_cols, source).reshape(8, 2), axis=1))
    args = (q, k, v, g, swaps, counts, seen_rows, seen_cols)
    if len(SIZES) == 1:
        return run_block(SIZES[0], *args)
    choice = sum((needed > 16 * n).astype(jnp.int32) for n in SIZES[:-1])
    return lax.switch(choice, [functools.partial(run_block, n) for n in SIZES], *args)


def solution(mesh):
    rows = P("dp", "seq", None, None)
    return jax.shard_map(
        shards,
        mesh=mesh,
        in_specs=(rows, rows, rows, rows, P(), P(), P(), P()),
        out_specs=(rows, rows, rows, rows),
        check_vma=False,
    )
```

```python
import functools

import jax
import jax.numpy as jnp
import numpy as np
from jax import lax
from jax.experimental import pallas as pl
from jax.experimental.pallas import tpu as pltpu
from jax.sharding import PartitionSpec as P

HEAD_DIM = 128
GRID_W = 32
CELLS = 512
FRAMES = 16
SLOTS = 2
WIDTH = 1536
PACK = 2 * HEAD_DIM
CHUNKS = WIDTH // PACK
SCALE = HEAD_DIM**-0.5
LOG2E = 1.4426950408889634
MASKED = -1e30
MESH = pl.DeviceIdType.MESH
BF16 = jnp.bfloat16
F32 = jnp.float32
TIME_AT = (3, 7, 11, 15, 17, 18)
SPACE_AT = (8, 11, 14, 17, 18, 19)
OFFSETS = (
    (1, 0), (3, 0), (0, 1), (0, 3), (1, 1), (3, 3), (1, 3), (3, 1),
    (2, 0), (0, 2), (2, 2), (1, 2), (3, 2), (2, 1), (2, 3),
)


def dot(a, b, dims):
    return lax.dot_general(a, b, (dims, ((), ())), preferred_element_type=F32)


def attend(q, k, v, g, bias):
    s = dot(q, k, ((1,), (1,))) * (SCALE * LOG2E) + bias
    e = jnp.exp2(s - jnp.max(s, axis=-1, keepdims=True))
    p = e * (1.0 / jnp.sum(e, axis=-1, keepdims=True))
    pb = p.astype(BF16)
    o = dot(pb, v, ((1,), (0,)))
    dv = dot(pb, g, ((0,), (0,)))
    dp = dot(g, v, ((1,), (1,)))
    row_dot = jnp.sum(p * dp, axis=-1, keepdims=True)
    ds = (p * (dp - row_dot) * SCALE).astype(BF16)
    dq = dot(ds, k, ((1,), (0,)))
    dk = dot(ds, q, ((0,), (0,)))
    return o, dq, dk, dv


@functools.cache
def reach():
    grid = [(y, x) for y in range(10, 17) for x in range(20, 33)]
    listed = {}
    for tall, broad in grid:
        y, x = np.divmod(np.arange(tall * broad), broad)
        listed[tall, broad] = y * GRID_W + x
    met = np.zeros((SLOTS * CELLS, SLOTS * CELLS), bool)
    for cells in listed.values():
        met[np.arange(cells.size), cells] = True
    second = np.zeros((CELLS, CELLS), bool)
    second |= met[:CELLS, :CELLS]
    for offset in {tall * broad for tall, broad in grid} | {256}:
        met[offset : offset + CELLS, CELLS:] |= second
    return met


def ranks(lo, hi):
    device = np.arange(16)
    x, y = device // 4, device % 4
    width = np.where((x + y) % 2 == 0, hi, lo)
    base = np.cumsum(width) - width
    cell = np.arange(hi)[None, :]
    rank = np.where(cell < width[:, None], base[:, None] + cell, -2)
    row = np.arange(2 * hi)
    cell_of = np.where(row < 2 * lo, row % lo, lo + (row - 2 * lo) % 8)
    cell_of = np.tile(cell_of.reshape(hi // 8, 1, 16), (1, FRAMES, 1)).reshape(hi // 8, 256)
    return rank.reshape(-1).astype(np.int32), cell_of.astype(np.int32)


def spans(met):
    found = []
    for k in range(0, met.shape[1], 256):
        end = min(k + 256, met.shape[1])
        hit = np.flatnonzero(met[:, k:end].any(axis=1))
        if hit.size:
            first = int(hit[0]) // 128 * 128
            last = min(-(-int(hit[-1] + 1) // 128) * 128, met.shape[0])
            found.append((k, end, first, last))
    return found


def select(one_hot, values, found):
    height = one_hot.shape[0]
    parts = [
        (first, last, dot(one_hot[first:last, k:end], values[k:end], ((1,), (0,))))
        for k, end, first, last in found
    ]
    blocks = []
    for r in range(0, height, 128):
        top = min(r + 128, height)
        terms = [p[r - first : top - first] for first, last, p in parts if first <= r < last]
        blocks.append(functools.reduce(lambda m, n: m + n, terms))
    return jnp.concatenate(blocks, axis=0)


def block_kernel(
    lo, hi,
    q_hbm, k_hbm, v_hbm, g_hbm,
    count_ref, rows_ref, cols_ref, flag_ref, rank_col, rank_row, cell_ref,
    out_hbm, back, tally,
    own, z_out, z_in, moved, grad, grad_out, stage, work, back_in, space, result,
    pack, unpack, z_pack, z_unpack, row_ref, space_bias, time_bias, diag_ref,
    z_send, z_recv, own_sem, grad_sem, gs_send, f_send, f_recv, b_send, b_recv, back_sem, out_sem,
):
    rows = 2 * hi
    cap = 16 * hi
    z_cap = 8 * (lo + hi)
    mixed = lo != hi
    raw = hi == 64
    place = ranks(lo, hi)[0]
    met = reach()[np.maximum(place, 0)] & (place >= 0)[:, None]
    pack_spans, unpack_spans = spans(met), spans(met.T)
    z_met = reach()[:z_cap]
    z_pack_spans, z_unpack_spans = spans(z_met), spans(z_met.T)
    me = lax.axis_index("seq")
    group = lax.axis_index("dp")
    partner = lax.rem(group + 4, 8)
    mx, my = me // 4, lax.rem(me, 4)
    wide = lax.rem(mx + my, 2) == 0
    peers = [
        (lax.rem(mx + ox, 4) * 4 + lax.rem(my + oy, 4), (ox + oy) % 2 == 0) for ox, oy in OFFSETS
    ]
    homes = (q_hbm, k_hbm, v_hbm)

    def by_width(do):
        if not mixed:
            do(hi, hi)
            return

        @pl.when(wide)
        def _():
            do(hi, lo)

        @pl.when(jnp.logical_not(wide))
        def _():
            do(lo, hi)

    def columns(i):
        return pl.ds(pl.multiple_of(i * PACK, PACK), PACK)

    def wait_bytes(ref, sem):
        pltpu.make_async_copy(ref, ref, sem).wait()

    def wait_rows(count, sem):
        wait_bytes(tally.at[pl.ds(0, count)], sem)

    def load_own(i, a):
        slot = lax.rem(i, 3)
        pltpu.make_async_copy(
            homes[a].at[:, :, columns(i)], own.at[slot, a], own_sem.at[slot, a]
        ).start()

    def send_swap(i, a):
        slot, kept = lax.rem(i, 2), lax.rem(i, 3)
        wait_bytes(own.at[kept, a], own_sem.at[kept, a])
        if not raw:
            values = own[kept, a].reshape(SLOTS * CELLS, PACK)
            z_out[slot, a] = select(z_pack, values, z_pack_spans).astype(BF16)
        pltpu.make_async_remote_copy(
            src_ref=own.at[kept, a] if raw else z_out.at[slot, a],
            dst_ref=z_in.at[i, a],
            send_sem=z_send.at[i, a],
            recv_sem=z_recv.at[i, a],
            device_id={"dp": partner},
            device_id_type=MESH,
        ).start()

    def packed(values):
        taken = select(pack, values, pack_spans)
        parts = [taken[:, b * 128 : (b + 1) * 128].reshape(16, hi, 128) for b in range(2)]
        if mixed:
            parts = [p[:, :lo] for p in parts] + [p[:, lo:] for p in parts]
        return jnp.concatenate(parts, axis=1).astype(BF16)

    def send_grad(i):
        wait_bytes(grad.at[i], grad_sem.at[i])
        grad_out[i] = packed(grad[i].reshape(SLOTS * CELLS, PACK))

        def send(mine, other):
            for peer, alike in peers:
                at = pl.ds(0, 2 * (mine if alike else other))
                pltpu.make_async_remote_copy(
                    src_ref=grad_out.at[i, peer, at],
                    dst_ref=work.at[i, me, 3, at],
                    send_sem=gs_send.at[i],
                    recv_sem=f_recv.at[i],
                    device_id={"seq": peer},
                    device_id_type=MESH,
                ).start()

        by_width(send)
        work[i, me, 3] = grad_out[i, me]

    def send_array(i, a):
        slot, kept = lax.rem(i, 2), lax.rem(i, 3)
        wait_bytes(z_in.at[i, a], z_recv.at[i, a])

        @pl.when(i >= 2)
        def _():
            by_width(lambda mine, other: wait_rows(2 * (7 * mine + 8 * other), f_send.at[slot, a]))

        if not raw:
            arrived = select(z_unpack, z_in[i, a], z_unpack_spans).astype(BF16)
        for s in range(SLOTS):
            part = z_in[i, a, s] if raw else arrived[s * CELLS : (s + 1) * CELLS]
            moved[kept, a, s] = jnp.where(flags[s] == 1, part, own[kept, a, s])
        stage[slot, a] = packed(moved[kept, a].reshape(SLOTS * CELLS, PACK))

        def send(mine, other):
            for peer, alike in peers:
                at = pl.ds(0, 2 * (mine if alike else other))
                pltpu.make_async_remote_copy(
                    src_ref=stage.at[slot, a, peer, at],
                    dst_ref=work.at[i, me, a, at],
                    send_sem=f_send.at[slot, a],
                    recv_sem=f_recv.at[i],
                    device_id={"seq": peer},
                    device_id_type=MESH,
                ).start()

        by_width(send)
        work[i, me, a] = stage[slot, a, me]
        wait_bytes(z_in.at[i, a], z_send.at[i, a])

        @pl.when(i + 3 < CHUNKS)
        def _():
            load_own(i + 3, a)

        @pl.when(i + 2 < CHUNKS)
        def _():
            send_swap(i + 2, a)

    def time_chunk(i):
        by_width(lambda mine, other: wait_rows(15 * 8 * mine, f_recv.at[i]))

        def one(r, _):
            at = pl.ds(pl.multiple_of(r * 16, 16), 16)
            q, k, v, g = [work[i, :, a, at, :].reshape(256, 128) for a in range(4)]
            bias = diag_ref[...] + time_bias[pl.ds(r, 1), :]
            for a, value in enumerate(attend(q, k, v, g, bias)):
                work[i, :, a, at, :] = value.astype(BF16).reshape(16, 16, 128)
            return 0

        steps = jnp.where(wide, hi // 8, lo // 8) if mixed else hi // 8
        lax.fori_loop(0, steps, one, 0)

        def send(mine, other):
            at = pl.ds(0, 2 * mine)
            for peer, _ in peers:
                pltpu.make_async_remote_copy(
                    src_ref=work.at[i, peer, :, at],
                    dst_ref=back.at[i, me, :, at],
                    send_sem=b_send.at[i],
                    recv_sem=b_recv.at[i],
                    device_id={"seq": peer},
                    device_id_type=MESH,
                ).start()
            pltpu.make_async_copy(work.at[i, me, :, at], back.at[i, me, :, at], b_recv.at[i]).start()

        by_width(send)

    def space_chunk(i):
        kept = lax.rem(i, 3)

        def one(step, _):
            s, b = step // 2, lax.rem(step, 2)
            lanes = pl.ds(pl.multiple_of(b * 128, 128), 128)
            q, k, v = [moved[kept, a, s, :, lanes] for a in range(3)]
            seen = row_ref[s]
            g = grad[i, s, :, lanes] * seen
            o, dq, dk, dv = attend(q, k, v, g, space_bias[s, 0:1, :])
            o = o * seen.astype(F32)
            for a, value in enumerate((o, dq, dk, dv)):
                space[a, s, :, lanes] = value
            return 0

        lax.fori_loop(0, 2 * SLOTS, one, 0)
        wait_rows(64 * (lo + hi), b_recv.at[i])
        fetch = pltpu.make_async_copy(back.at[i], back_in, back_sem)
        fetch.start()
        fetch.wait()

        @pl.when(i > 0)
        def _():
            wait_bytes(result, out_sem)

        for a in range(4):
            value = back_in[:, a].astype(F32)
            if mixed:
                base = [value[:, b * lo : (b + 1) * lo] for b in range(2)]
                extra = value[:, 2 * lo :]
                device = lax.broadcasted_iota(jnp.int32, extra.shape, 0)
                extra = jnp.where(((device >> 2) + device) & 1 == 0, extra, 0.0)
                parts = [jnp.concatenate([base[b], extra[:, b * 8 : (b + 1) * 8]], 1) for b in range(2)]
            else:
                parts = [value[:, b * hi : (b + 1) * hi] for b in range(2)]
            parts = [p.reshape(cap, 128) for p in parts]
            taken = select(unpack, jnp.concatenate(parts, axis=1).astype(BF16), unpack_spans)
            summed = space[a].reshape(SLOTS * CELLS, PACK) + taken
            result[a] = summed.astype(BF16).reshape(SLOTS, CELLS, PACK)
        for a in range(4):
            pltpu.make_async_copy(result.at[a], out_hbm.at[a, :, :, columns(i)], out_sem).start()

    barrier = pltpu.get_barrier_semaphore()
    for peer, _ in peers:
        pl.semaphore_signal(barrier, inc=1, device_id={"seq": peer}, device_id_type=MESH)
    pl.semaphore_signal(barrier, inc=1, device_id={"dp": partner}, device_id_type=MESH)
    for i in range(3):
        for a in range(3):
            load_own(i, a)

    def load_grad(i, _):
        pltpu.make_async_copy(g_hbm.at[:, :, columns(i)], grad.at[i], grad_sem.at[i]).start()
        return 0

    lax.fori_loop(0, CHUNKS, load_grad, 0)

    flags = [flag_ref[lax.rem(group, 4) * 2 + s] for s in range(SLOTS)]

    def extents(ref):
        here = [ref[group * 2 + s] for s in range(SLOTS)]
        there = [ref[partner * 2 + s] for s in range(SLOTS)]
        return here, [jnp.where(flags[s] == 1, there[s], here[s]) for s in range(SLOTS)]

    home_counts, counts = extents(count_ref)
    home_rows, seen_rows = extents(rows_ref)
    home_cols, seen_cols = extents(cols_ref)
    areas = [seen_rows[s] * seen_cols[s] for s in range(SLOTS)]

    def places(index, extent_counts, extent_rows, extent_cols, first, second):
        later = index >= CELLS
        y, x = (index & (CELLS - 1)) >> 5, index & (GRID_W - 1)
        tall = jnp.where(later, extent_rows[1], extent_rows[0])
        broad = jnp.where(later, extent_cols[1], extent_cols[0])
        count = jnp.where(later, extent_counts[1], extent_counts[0])
        live = (y < tall) & (x < broad) & (me < count) & (jnp.where(later, second[1], first[1]) == 1)
        return jnp.where(live, jnp.where(later, second[0], first[0]) + y * broad + x, -1)

    across = lax.broadcasted_iota(jnp.int32, (1, SLOTS * CELLS), 1)
    along = lax.broadcasted_iota(jnp.int32, (SLOTS * CELLS, 1), 0)
    home_area = jnp.where(flags[0] == 1, home_rows[0] * home_cols[0], 256)
    target_area = jnp.where(flags[0] == 1, areas[0], 256)
    here = (counts, seen_rows, seen_cols)

    def one_hot(a, b):
        return jnp.where(a == b, 1.0, 0.0).astype(BF16)

    leaving = places(across, home_counts, home_rows, home_cols, (0, flags[0]), (home_area, flags[1]))
    pack[...] = one_hot(rank_col[...], places(across, *here, (0, 1), (areas[0], 1)))
    pl.semaphore_wait(barrier, 16)
    send_grad(0)
    if not raw:
        z_pack[...] = one_hot(lax.broadcasted_iota(jnp.int32, (z_cap, 1), 0), leaving)
    for a in range(3):
        send_swap(jnp.int32(0), a)
    send_grad(1)
    for a in range(3):
        send_swap(jnp.int32(1), a)

    def more_grads(i, _):
        send_grad(i)
        return 0

    lax.fori_loop(2, CHUNKS, more_grads, 0)
    arriving = places(along, *here, (0, flags[0]), (target_area, flags[1]))
    if not raw:
        z_unpack[...] = one_hot(arriving, lax.broadcasted_iota(jnp.int32, (1, z_cap), 1))
    landing = places(along, *here, (0, 1), (areas[0], 1))
    unpack[...] = one_hot(landing, rank_row[0:1, :])
    for s in range(SLOTS):
        part = landing[s * CELLS : (s + 1) * CELLS]
        row_ref[s] = jnp.broadcast_to(jnp.where(part >= 0, 1.0, 0.0), (CELLS, 128)).astype(BF16)
        cell = lax.broadcasted_iota(jnp.int32, (8, CELLS), 1)
        live = ((cell >> 5) < seen_rows[s]) & ((cell & (GRID_W - 1)) < seen_cols[s])
        space_bias[s] = jnp.where(live & (me < counts[s]), 0.0, MASKED)
    cell = cell_ref[...]
    rank = me * lo + cell + (hi - lo) * (2 * mx + (my + 1 - lax.rem(mx, 2)) // 2)
    count = jnp.where(rank < areas[0], counts[0], counts[1])
    count = jnp.where(rank < areas[0] + areas[1], count, FRAMES)
    frame = lax.broadcasted_iota(jnp.int32, cell.shape, 1) >> 4
    time_bias[...] = jnp.where(frame < count, 0.0, MASKED)
    first = lax.broadcasted_iota(jnp.int32, (256, 256), 0)
    second = lax.broadcasted_iota(jnp.int32, (256, 256), 1)
    diag_ref[...] = jnp.where((first & 15) == (second & 15), 0.0, MASKED)

    def done_by(u, times):
        return sum((u >= time).astype(jnp.int32) for time in times)

    def stage_of(u, times, do):
        def one(i, _):
            do(i)
            return 0

        lax.fori_loop(done_by(u - 1, times), done_by(u, times), one, 0)

    def step(i, _):
        for a in range(3):
            u = 3 * i + a

            @pl.when(i < CHUNKS)
            def _():
                send_array(i, a)

            stage_of(u, TIME_AT, time_chunk)
            stage_of(u, SPACE_AT, space_chunk)
        return 0

    lax.fori_loop(0, CHUNKS + 1, step, 0)
    wait_bytes(result, out_sem)

    def finish(i, _):
        def sent(mine, other):
            wait_rows(2 * (7 * mine + 8 * other), gs_send.at[i])
            wait_rows(15 * 8 * mine, b_send.at[i])

        by_width(sent)
        return 0

    lax.fori_loop(0, CHUNKS, finish, 0)
    for i in range(2):
        for a in range(3):
            by_width(lambda mine, other: wait_rows(2 * (7 * mine + 8 * other), f_send.at[i, a]))


def run_block(lo, hi, q, k, v, g, *tables):
    rows, cap, z_cap = 2 * hi, 16 * hi, 8 * (lo + hi)
    rank, cell_of = ranks(lo, hi)
    shape = (SLOTS, CELLS, WIDTH)
    pair = (SLOTS, CELLS, PACK)
    raw = hi == 64
    z_one = pair if raw else (z_cap, PACK)
    z_rows = 16 if raw else z_cap
    whole = pl.BlockSpec(memory_space=pl.ANY)
    local = pl.BlockSpec(memory_space=pltpu.VMEM)
    scalar = pl.BlockSpec(memory_space=pltpu.SMEM)
    dma = pltpu.SemaphoreType.DMA
    outs = pl.pallas_call(
        functools.partial(block_kernel, lo, hi),
        out_shape=[
            jax.ShapeDtypeStruct((4,) + shape, BF16),
            jax.ShapeDtypeStruct((CHUNKS, 16, 4, rows, 128), BF16),
            jax.ShapeDtypeStruct((128 * hi, 128), BF16),
        ],
        in_specs=[whole] * 4 + [scalar] * 4 + [local] * 3,
        out_specs=[whole] * 3,
        scratch_shapes=[
            pltpu.VMEM((3, 3) + pair, BF16),
            pltpu.VMEM((2, 3, z_rows, PACK), BF16),
            pltpu.VMEM((CHUNKS, 3) + z_one, BF16),
            pltpu.VMEM((3, 3) + pair, BF16),
            pltpu.VMEM((CHUNKS,) + pair, BF16),
            pltpu.VMEM((CHUNKS, 16, rows, 128), BF16),
            pltpu.VMEM((2, 3, 16, rows, 128), BF16),
            pltpu.VMEM((CHUNKS, 16, 4, rows, 128), BF16),
            pltpu.VMEM((16, 4, rows, 128), BF16),
            pltpu.VMEM((4,) + pair, F32),
            pltpu.VMEM((4,) + pair, BF16),
            pltpu.VMEM((cap, SLOTS * CELLS), BF16),
            pltpu.VMEM((SLOTS * CELLS, cap), BF16),
            pltpu.VMEM((z_rows, SLOTS * CELLS), BF16),
            pltpu.VMEM((SLOTS * CELLS, z_rows), BF16),
            pltpu.VMEM((SLOTS, CELLS, 128), BF16),
            pltpu.VMEM((SLOTS, 8, CELLS), F32),
            pltpu.VMEM((hi // 8, 256), F32),
            pltpu.VMEM((256, 256), F32),
            dma((CHUNKS, 3)),
            dma((CHUNKS, 3)),
            dma((3, 3)),
            dma((CHUNKS,)),
            dma((CHUNKS,)),
            dma((2, 3)),
            dma((CHUNKS,)),
            dma((CHUNKS,)),
            dma((CHUNKS,)),
            dma,
            dma,
        ],
        compiler_params=pltpu.CompilerParams(
            collective_id=(lo + hi) // 8, has_side_effects=True, vmem_limit_bytes=63 * 2**20
        ),
        cost_estimate=pl.CostEstimate(
            flops=4 * 10**10, bytes_accessed=48 * 2**20, transcendentals=10**7
        ),
    )(
        *[value.reshape(shape) for value in (q, k, v, g)],
        *tables,
        rank.reshape(cap, 1),
        np.tile(rank, (8, 1)),
        cell_of,
    )
    return outs[0].reshape(4, SLOTS, 1, CELLS, WIDTH)


SIZES = ((48, 48), (56, 56), (64, 64))


def shards(q, k, v, g, frame_counts, patch_rows, patch_cols, swap_flags):
    flags = jnp.concatenate([swap_flags, swap_flags]).reshape(16)
    areas = patch_rows * patch_cols
    areas = jnp.where(flags == 1, jnp.roll(areas, 8), areas)
    needed = jnp.max(jnp.sum(areas.reshape(8, SLOTS), axis=1))
    args = (q, k, v, g, frame_counts, patch_rows, patch_cols, swap_flags.reshape(8))
    if len(SIZES) == 1:
        done = run_block(*SIZES[0], *args)
        return tuple(done[a] for a in range(4))
    choice = sum((needed > 8 * (lo + hi)).astype(jnp.int32) for lo, hi in SIZES[:-1])
    done = lax.switch(choice, [functools.partial(run_block, lo, hi) for lo, hi in SIZES], *args)
    return tuple(done[a] for a in range(4))


def solution(mesh):
    rows = P("dp", "seq", None, None)
    return jax.shard_map(
        shards,
        mesh=mesh,
        in_specs=(rows, rows, rows, rows, P(), P(), P(), P()),
        out_specs=(rows, rows, rows, rows),
        check_vma=False,
    )
```
